128 devices in a mesh: dp: 4 (over x_lo, core), comp: 32 (over z, x_hi, y).
Axes of the slice: x: 4 (x_hi: 2, x_lo: 2; x = x_hi * 2 + x_lo), y: 4, z: 4, core: 2. Of those that a mesh axis runs over, the one named last changes fastest.
Arguments:
- embeddings: bfloat16 [12288, 1024], P(('dp', 'comp')), may hold values from -64 to 64
- centroids: bfloat16 [65536, 1024], P('comp'), may hold values from -64 to 64
Outputs:
- new_centroids: bfloat16 [65536, 1024], P('comp', 'dp')
- soft_counts: float32 [65536], P('comp')
- log_totals: float32 [12288], P(('dp', 'comp'))
The draws below stay inside these ranges and needn't reach their ends.
All inputs are finite; a program needn't handle non-finite values.
Results may differ from the reference program's by a relative error of at most 0.0034.
Values may be sent and summed in bfloat16 or wider, within the bound.
A program may use at most 128 MiB of HBM per device.

```python
import jax
import jax.numpy as jnp
from jax import lax

D = 1024
K = 65536
ROWS = 12288
BLOCK_ROWS = 768


def shared_centres(key):
    region_key, cluster_key = jax.random.split(key)
    regions = jax.random.normal(region_key, (8, D), jnp.float32)
    clusters = jax.random.normal(cluster_key, (K // 32, D), jnp.float32)
    return (regions, clusters)


def compose(regions, clusters, cluster_ids, spread, jitter, scales):
    region_ids = cluster_ids % 8
    total = 0.6 * jnp.take(regions, region_ids, axis=0) + jnp.take(clusters, cluster_ids, axis=0) + spread * jitter
    return jnp.clip(total * scales, -64.0, 64.0)


def draw_embeddings(key, part):
    regions, clusters = shared_centres(key)
    key = jax.random.fold_in(key, 1)
    cluster_key, spread_key, jitter_key, scale_key = jax.random.split(key, 4)
    cluster_ids = jax.random.randint(cluster_key, (ROWS,), 0, K // 32)
    spread = jax.random.uniform(spread_key, (ROWS, 1), jnp.float32, 0.3, 0.8)
    jitter = jax.random.normal(jitter_key, (ROWS, D), jnp.float32)
    scales = jnp.exp(0.3 * jax.random.normal(scale_key, (ROWS, 1), jnp.float32))
    return compose(regions, clusters, cluster_ids, spread, jitter, scales).astype(jnp.bfloat16)


def draw_centroids(key, part):
    regions, clusters = shared_centres(key)
    key = jax.random.fold_in(key, 2)
    first_key, second_key, jitter_key, scale_key = jax.random.split(key, 4)
    first_ids = jax.random.randint(first_key, (K,), 0, K // 32)
    second_ids = jax.random.randint(second_key, (K,), 0, K // 32)
    cluster_ids = jnp.minimum(first_ids, second_ids)
    jitter = jax.random.normal(jitter_key, (K, D), jnp.float32)
    scales = jnp.exp(0.3 * jax.random.normal(scale_key, (K, 1), jnp.float32))
    return compose(regions, clusters, cluster_ids, 0.35, jitter, scales).astype(jnp.bfloat16)


def setup_inputs(seed: int = 0) -> dict:
    key_of = jax.random.split(jax.random.key(seed), 3)
    return {
        "embeddings": draw_embeddings(jax.random.fold_in(key_of[2], 71), 0),
        "centroids": draw_centroids(jax.random.fold_in(key_of[2], 71), 0),
    }


def unit_rows(values):
    floats = values.astype(jnp.float32)
    return (floats * lax.rsqrt(lax.optimization_barrier(jnp.sum(floats * floats, axis=1, keepdims=True)) + 1e-06)).astype(jnp.bfloat16)

def reference(embeddings, centroids):
    rows_unit = unit_rows(embeddings)
    centroid_unit = unit_rows(centroids)
    blocks = rows_unit.reshape(ROWS // BLOCK_ROWS, BLOCK_ROWS, D)

    def one_block(running, row_block):
        weighted, counts = running
        scores = lax.dot_general(row_block, centroid_unit, (((1,), (1,)), ((), ())), preferred_element_type=jnp.float32)
        probs = jnp.exp(scores * 10.0 - 10.0)
        totals = lax.optimization_barrier(jnp.sum(probs, axis=1))
        weights = (probs / totals[:, None]).astype(jnp.bfloat16)
        weighted = weighted + lax.dot_general(weights, row_block, (((0,), (0,)), ((), ())), preferred_element_type=jnp.float32)
        counts = counts + lax.optimization_barrier(jnp.sum(weights.astype(jnp.float32), axis=0))
        return ((weighted, counts), jnp.log(totals) + 10.0)
    start = (jnp.zeros((K, D), jnp.float32), jnp.zeros((K,), jnp.float32))
    (weighted, counts), log_totals = lax.scan(one_block, start, blocks)
    squares = lax.optimization_barrier(jnp.sum(weighted * weighted, axis=1, keepdims=True))
    new_centroids = (weighted * lax.rsqrt(squares + 1e-06)).astype(jnp.bfloat16)
    return (new_centroids, counts, log_totals.reshape(ROWS))
```

```python
import jax
import jax.numpy as jnp
from jax import lax
from jax.experimental import pallas as pl
from jax.experimental.pallas import tpu as pltpu
from jax.sharding import PartitionSpec as P

MESH = pl.DeviceIdType.MESH
F32 = jnp.float32
BF16 = jnp.bfloat16

ORDER = (
    (0, 0), (1, 0), (0, 1), (3, 0), (0, 3), (2, 0), (0, 2), (1, 1),
    (3, 3), (1, 3), (3, 1), (2, 1), (1, 2), (2, 3), (3, 2), (2, 2),
)
SLOTS = len(ORDER)
SLOT_OF = {place: slot for slot, place in enumerate(ORDER)}
NODE = 128
HALF = NODE // 2
STEP = 2 * NODE
BATCH = SLOTS * STEP
ROWS_A = 64
ROWS_B = 32
NEXT_BATCH_AT = 12


def children(slot, half):
    place = ORDER[slot]
    first, second = place if half == 0 else place[::-1]
    found = []
    if second == 0:
        if first == 0:
            found += [((1, 0), 0, 1), ((3, 0), 0, -1)]
        if first == 1:
            found += [((2, 0), 0, 1)]
        found += [((first, 1), 1, 1), ((first, 3), 1, -1)]
    elif second == 1 and first in (0, 1):
        found += [((first, 2), 1, 1)]
    elif second == 3 and first in (2, 3):
        found += [((first, 2), 1, -1)]
    if half == 0:
        return [(SLOT_OF[p], axis, way) for p, axis, way in found]
    return [(SLOT_OF[p[::-1]], 1 - axis, way) for p, axis, way in found]


def kernel(
    emb_hbm, cent_hbm, out_hbm, count_out, log_out,
    rows, probs, cent, emb, own_sum, sum_send, sum_recv, final,
    part_src, part_dst, x_src, x_dst, inv, inv_src, count, count_src, count_dst, count_all, sq_src, sq_dst,
    load_sem, row_send, row_recv, sib_send, sib_recv, pre_send, pre_recv,
    part_send, part_recv, xs_send, xs_recv, inv_send, inv_recv,
    sum_ssem, sum_rsem, cnt_send, cnt_recv, sq_send, sq_recv, out_sem, out_send, out_recv, all_send, all_recv,
):
    dp = lax.axis_index("dp")
    comp = lax.axis_index("comp")
    core = lax.rem(dp, 2)
    other = 1 - core
    x_lo = dp // 2
    y = lax.rem(comp, 4)
    x = lax.rem(comp // 4, 2) * 2 + x_lo
    z = comp // 8
    sign = 1 - 2 * core

    def device(dx, dy, dz, dcore):
        nx = lax.rem(x + dx + 4, 4)
        ny = lax.rem(y + dy + 4, 4)
        nz = lax.rem(z + dz + 4, 4)
        ncore = lax.rem(core + dcore, 2)
        return {"dp": lax.rem(nx, 2) * 2 + ncore, "comp": nz * 8 + (nx // 2) * 4 + ny}

    def remote(src, dst, ssem, rsem, target):
        return pltpu.make_async_remote_copy(
            src_ref=src, dst_ref=dst, send_sem=ssem, recv_sem=rsem, device_id=target, device_id_type=MESH
        )

    def wait_bytes(ref, sem):
        pltpu.make_async_copy(ref, ref, sem).wait()

    sibling = device(0, 0, 0, 1)
    x_far = device(2, 0, 0, 0)
    x_pair = device(1 - 2 * x_lo, 0, 0, 0)

    barrier = pltpu.get_barrier_semaphore()
    greeted = 0
    for dy, dz in ORDER:
        for dcore in (0, 1):
            if (dy, dz, dcore) != (0, 0, 0):
                pl.semaphore_signal(barrier, inc=1, device_id=device(0, dy, dz, dcore), device_id_type=MESH)
                greeted += 1
    for dx in (1, 2, 3):
        pl.semaphore_signal(barrier, inc=1, device_id=device(dx, 0, 0, 0), device_id_type=MESH)
        greeted += 1

    emb_copy = pltpu.make_async_copy(emb_hbm, emb, load_sem.at[0])
    emb_copy.start()
    cent_copy = pltpu.make_async_copy(cent_hbm.at[pl.ds(core * 1024, 1024)], cent, load_sem.at[1])
    cent_copy.start()

    def unit(values):
        floats = values.astype(F32)
        return (floats * lax.rsqrt(jnp.sum(floats * floats, axis=1, keepdims=True) + 1e-06)).astype(BF16)

    emb_copy.wait()
    rows[0, pl.ds(0, ROWS_A), :] = unit(emb[pl.ds(0, ROWS_A), :])
    rows[1, pl.ds(0, ROWS_B), :] = unit(emb[pl.ds(ROWS_A, ROWS_B), :])
    pl.semaphore_wait(barrier, greeted)

    def pre(batch, size, chunk, dx):
        return remote(
            rows.at[batch, pl.ds(0, size)],
            rows.at[batch, pl.ds(chunk * size, size)],
            pre_send.at[batch, chunk],
            pre_recv.at[batch, chunk],
            device(-dx, 0, 0, 0),
        )

    pres = [pre(0, ROWS_A, 1, 2)] + [pre(1, ROWS_B, j, j) for j in (1, 2, 3)]
    pres[0].start()

    def row_copy(batch, slot, half, child, axis, way):
        dy, dz = (way * sign, 0) if axis == 0 else (0, way * sign)
        return remote(
            rows.at[batch, pl.ds(slot * STEP + half * HALF, HALF)],
            rows.at[batch, pl.ds(child * STEP + half * HALF, HALF)],
            row_send.at[batch],
            row_recv.at[batch, child, half],
            device(0, dy, dz, 0),
        )

    def hand_on(batch, slot, half):
        for child, axis, way in children(slot, half):
            row_copy(batch, slot, half, child, axis, way).start()

    def to_sibling(batch, slot):
        return remote(
            rows.at[batch, pl.ds(slot * STEP, NODE)],
            rows.at[batch, pl.ds(slot * STEP + NODE, NODE)],
            sib_send.at[batch],
            sib_recv.at[batch, slot],
            sibling,
        )

    def arrive(batch, slot):
        for half in (0, 1):
            row_copy(batch, slot, half, slot, 0, 1).wait_recv()
            hand_on(batch, slot, half)
        to_sibling(batch, slot).start()

    hand_on(0, 0, 0)
    for copy in pres[1:]:
        copy.start()
    pres[0].wait_recv()
    hand_on(0, 0, 1)
    to_sibling(0, 0).start()

    cent_copy.wait()

    def unit_block(i, carry):
        block = pl.ds(i * 128, 128)
        cent[block, :] = unit(cent[block, :])
        return carry

    lax.fori_loop(0, 8, unit_block, 0)
    for copy in pres[1:]:
        copy.wait_recv()

    def score(batch, slot):
        block = rows[batch, pl.ds(slot * STEP, STEP), :]
        scores = lax.dot_general(cent[...], block, (((1,), (1,)), ((), ())), preferred_element_type=F32)
        p = jnp.exp(scores * 10.0 - 10.0)
        probs[batch, :, pl.ds(slot * STEP, STEP)] = p.astype(BF16)
        part = jnp.sum(p.reshape(128, 8, STEP), axis=0)
        part_src[batch, 2 * slot] = part[:, :NODE]
        part_src[batch, 2 * slot + 1] = part[:, NODE:]

    def send_part(batch, slot):
        dy, dz = ORDER[slot]
        if slot > 0:
            remote(
                part_src.at[batch, 2 * slot], part_dst.at[batch, 2 * slot], part_send.at[batch], part_recv.at[batch],
                device(0, -sign * dy, -sign * dz, 0),
            ).start()
        else:
            part_dst[batch, 0] = part_src[batch, 0]
        remote(
            part_src.at[batch, 2 * slot + 1], part_dst.at[batch, 2 * slot + 1], part_send.at[batch], part_recv.at[batch],
            device(0, sign * dy, sign * dz, 1),
        ).start()

    def x_copy(batch):
        return remote(x_src.at[batch], x_dst.at[batch], xs_send.at[batch], xs_recv.at[batch], x_far)

    def totals_first(batch):
        wait_bytes(part_dst.at[batch, pl.ds(1, 2 * SLOTS - 1)], part_recv.at[batch])
        x_src[batch] = jnp.sum(part_dst[batch], axis=0)
        x_copy(batch).start()

    def totals_second(batch):
        x_copy(batch).wait_recv()
        tile = x_src[batch] + pltpu.roll(x_dst[batch], HALF, 1)
        total = jnp.broadcast_to(jnp.sum(tile, axis=0, keepdims=True), (8, NODE))
        inv_src[batch] = 1.0 / total
        inv[batch, 0] = 1.0 / total
        for slot, (dy, dz) in enumerate(ORDER):
            for dcore in (0, 1):
                if slot + dcore > 0:
                    remote(
                        inv_src.at[batch], inv.at[batch, 2 * slot + dcore], inv_send.at[batch], inv_recv.at[batch],
                        device(0, sign * dy, sign * dz, dcore),
                    ).start()
        return jnp.log(total) + 10.0

    def totals_third(batch):
        wait_bytes(inv.at[batch, pl.ds(1, 2 * SLOTS - 1)], inv_recv.at[batch])

    def scale(batch, m):
        def block(i, carry):
            at = pl.ds(m * 512 + i * 64, 64)
            total = jnp.zeros((64, NODE), F32)
            for tile in range(2 * SLOTS):
                lanes = pl.ds(tile * NODE, NODE)
                weights = (probs[batch, at, lanes].astype(F32) * inv[batch, tile, 0:1, :]).astype(BF16)
                probs[batch, at, lanes] = weights
                total = total + weights.astype(F32)
            count[at, :] = total
            return carry

        lax.fori_loop(0, 8, block, 0)

    def to_row(block):
        return jnp.sum(block.T, axis=0, keepdims=True)

    def weighted(batch, m, column):
        return lax.dot_general(
            probs[batch, pl.ds(m * 512, 512), :],
            rows[batch, :, pl.ds(column, 512)],
            (((1,), (0,)), ((), ())),
            preferred_element_type=F32,
        )

    def sum_copy(m):
        at = pl.ds(m * 512, 512)
        return remote(sum_send.at[at], sum_recv.at[at], sum_ssem.at[m], sum_rsem.at[m], x_pair)

    def count_copy():
        return remote(count_src.at[0], count_dst, cnt_send, cnt_recv, x_pair)

    def count_rows(batch, m):
        def one(i, carry):
            r = m * 4 + i
            count_src[batch, pl.ds(r, 1), :] = to_row(count[pl.ds(r * 128, 128), :])
            return carry

        lax.fori_loop(0, 4, one, 0)

    def step(t, carry):
        batch = t // SLOTS
        slot = lax.rem(t, SLOTS)
        ahead = (t + 1) // SLOTS
        for k in range(1, SLOTS):
            @pl.when(lax.rem(t + 1, SLOTS) == k)
            def _():
                arrive(ahead, k)

        @pl.when(t == NEXT_BATCH_AT)
        def _():
            hand_on(1, 0, 0)
            hand_on(1, 0, 1)
            to_sibling(1, 0).start()

        to_sibling(batch, slot).wait_recv()
        score(batch, slot)
        for k in range(SLOTS):
            @pl.when(slot == k)
            def _():
                send_part(batch, k)

        @pl.when(t == SLOTS)
        def _():
            totals_first(0)

        @pl.when(t == SLOTS + 1)
        def _():
            logs = totals_second(0)
            log_out[0:1, :] = logs[0:1]

        @pl.when(t == SLOTS + 3)
        def _():
            totals_third(0)

        @pl.when((t == SLOTS + 3) | (t == SLOTS + 4))
        def _():
            m = t - (SLOTS + 3)
            scale(0, m)
            at = pl.ds(m * 512, 512)
            sum_send[at, :] = weighted(0, m, (1 - x_lo) * 512).astype(BF16)
            sum_copy(m).start()
            count_rows(0, m)

        @pl.when(t == SLOTS + 5)
        def _():
            count_copy().start()

        @pl.when((t == SLOTS + 6) | (t == SLOTS + 8))
        def _():
            m = (t - (SLOTS + 6)) // 2
            own_sum[pl.ds(m * 512, 512), :] = weighted(0, m, x_lo * 512)

        return carry

    lax.fori_loop(0, 2 * SLOTS, step, 0)

    totals_first(1)
    logs = totals_second(1)
    log_out[1:2, :] = logs[0:1]
    totals_third(1)

    def sq_copy(m):
        return remote(sq_src.at[m], sq_dst.at[m], sq_send.at[m], sq_recv.at[m], x_pair)

    def finish(m, carry):
        at = pl.ds(m * 512, 512)
        scale(1, m)
        total = weighted(1, m, x_lo * 512) + own_sum[at, :]
        sum_copy(m).wait_recv()
        total = total + sum_recv[at, :].astype(F32)
        own_sum[at, :] = total
        squares = total * total
        lanes = squares[:, :128] + squares[:, 128:256] + squares[:, 256:384] + squares[:, 384:]
        sq_src[m] = jnp.concatenate(
            [to_row(lanes[i * 128 : (i + 1) * 128]) for i in range(4)] + [jnp.zeros((4, 128), F32)], axis=0
        )
        sq_copy(m).start()
        count_rows(1, m)
        return carry

    lax.fori_loop(0, 2, finish, 0)

    count_copy().wait_recv()
    mine = pl.ds(pl.multiple_of(core * 8, 8), 8)
    count_all[mine, :] = count_src[0] + count_dst[...] + count_src[1]
    all_copy = remote(count_all.at[mine], count_all.at[mine], all_send, all_recv, sibling)
    all_copy.start()

    def out_copies(m):
        at = pl.ds(m * 512, 512)
        place = pl.ds(core * 1024 + m * 512, 512)
        local = pltpu.make_async_copy(
            final.at[at, pl.ds(pl.multiple_of(core * 256, 256), 256)], out_hbm.at[place], out_sem.at[m]
        )
        away = remote(
            final.at[at, pl.ds(pl.multiple_of(other * 256, 256), 256)],
            out_hbm.at[place],
            out_send.at[m],
            out_recv.at[m],
            sibling,
        )
        return local, away

    def normalize(m, carry):
        sq_copy(m).wait_recv()

        def one(i, carry):
            at = pl.ds(m * 512 + i * 128, 128)
            squares = sq_src[m, pl.ds(i, 1), :] + sq_dst[m, pl.ds(i, 1), :]
            factor = jnp.broadcast_to(lax.rsqrt(squares + 1e-06), (128, 128)).T
            for tile in range(4):
                lanes = pl.ds(tile * 128, 128)
                final[at, lanes] = (own_sum[at, lanes] * factor).astype(BF16)
            return carry

        lax.fori_loop(0, 4, one, 0)
        local, away = out_copies(m)
        local.start()
        away.start()
        return carry

    lax.fori_loop(0, 2, normalize, 0)

    all_copy.wait()
    count_out[...] = count_all[...]
    for copy in pres:
        copy.wait_send()
    for batch in (0, 1):
        wait_bytes(rows.at[batch, pl.ds(0, (SLOTS - 1) * NODE)], row_send.at[batch])
        wait_bytes(rows.at[batch, pl.ds(0, SLOTS * NODE)], sib_send.at[batch])
        wait_bytes(part_dst.at[batch, pl.ds(1, 2 * SLOTS - 1)], part_send.at[batch])
        wait_bytes(inv.at[batch, pl.ds(1, 2 * SLOTS - 1)], inv_send.at[batch])
        x_copy(batch).wait_send()
    count_copy().wait_send()
    for m in (0, 1):
        sum_copy(m).wait_send()
        sq_copy(m).wait_send()
        local, away = out_copies(m)
        local.wait()
        away.wait()


def on_device(embeddings, centroids):
    dma = pltpu.SemaphoreType.DMA
    any_space = pl.BlockSpec(memory_space=pl.ANY)
    vmem = pl.BlockSpec(memory_space=pltpu.VMEM)
    new_centroids, counts, logs = pl.pallas_call(
        kernel,
        out_shape=(
            jax.ShapeDtypeStruct((2048, 256), BF16),
            jax.ShapeDtypeStruct((16, 128), F32),
            jax.ShapeDtypeStruct((2, 128), F32),
        ),
        in_specs=[any_space, any_space],
        out_specs=(any_space, vmem, vmem),
        scratch_shapes=[
            pltpu.VMEM((2, BATCH, 1024), BF16),
            pltpu.VMEM((2, 1024, BATCH), BF16),
            pltpu.VMEM((1024, 1024), BF16),
            pltpu.VMEM((96, 1024), BF16),
            pltpu.VMEM((1024, 512), F32),
            pltpu.VMEM((1024, 512), BF16),
            pltpu.VMEM((1024, 512), BF16),
            pltpu.VMEM((1024, 512), BF16),
            pltpu.VMEM((2, 2 * SLOTS, 8, NODE), F32),
            pltpu.VMEM((2, 2 * SLOTS, 8, NODE), F32),
            pltpu.VMEM((2, 8, NODE), F32),
            pltpu.VMEM((2, 8, NODE), F32),
            pltpu.VMEM((2, 2 * SLOTS, 8, NODE), F32),
            pltpu.VMEM((2, 8, NODE), F32),
            pltpu.VMEM((1024, NODE), F32),
            pltpu.VMEM((2, 8, 128), F32),
            pltpu.VMEM((8, 128), F32),
            pltpu.VMEM((16, 128), F32),
            pltpu.VMEM((2, 8, 128), F32),
            pltpu.VMEM((2, 8, 128), F32),
            dma((2,)),
            dma((2,)), dma((2, SLOTS, 2)),
            dma((2,)), dma((2, SLOTS)),
            dma((2, 4)), dma((2, 4)),
            dma((2,)), dma((2,)),
            dma((2,)), dma((2,)),
            dma((2,)), dma((2,)),
            dma((2,)), dma((2,)),
            dma, dma,
            dma((2,)), dma((2,)),
            dma((2,)), dma((2,)), dma((2,)),
            dma, dma,
        ],
        compiler_params=pltpu.CompilerParams(
            collective_id=0, has_side_effects=True, vmem_limit_bytes=60 * 1024 * 1024
        ),
        name="soft_kmeans",
    )(embeddings, centroids)
    log_totals = jnp.concatenate([logs[0, :ROWS_A], logs[1, :ROWS_B]])
    return new_centroids, counts.reshape(2048), log_totals


def solution(mesh):
    return jax.shard_map(
        on_device,
        mesh=mesh,
        in_specs=(P(("dp", "comp"), None), P("comp", None)),
        out_specs=(P("comp", "dp"), P("comp"), P(("dp", "comp"))),
        check_vma=False,
    )
```

```python
import jax
import jax.numpy as jnp
from jax import lax
from jax.experimental import pallas as pl
from jax.experimental.pallas import tpu as pltpu
from jax.sharding import PartitionSpec as P

MESH = pl.DeviceIdType.MESH
F32 = jnp.float32
BF16 = jnp.bfloat16

ORDER = (
    (0, 0), (1, 0), (0, 1), (3, 0), (0, 3), (2, 0), (0, 2), (1, 1),
    (3, 3), (1, 3), (3, 1), (2, 1), (1, 2), (2, 3), (3, 2), (2, 2),
)
SLOTS = len(ORDER)
SLOT_OF = {place: slot for slot, place in enumerate(ORDER)}
OWN = 96
EARLY = 64
NODE = 2 * OWN
HALF = (OWN + EARLY) // 2
STEP = 2 * NODE
ROWS = SLOTS * STEP
LEAD = 2
PART = 256
LUMP = 256
LUMPS = 1024 // LUMP


def children(slot, half):
    place = ORDER[slot]
    first, second = place if half == 0 else place[::-1]
    found = []
    if second == 0:
        if first == 0:
            found += [((1, 0), 0, 1), ((3, 0), 0, -1)]
        if first == 1:
            found += [((2, 0), 0, 1)]
        found += [((first, 1), 1, 1), ((first, 3), 1, -1)]
    elif second == 1 and first in (0, 1):
        found += [((first, 2), 1, 1)]
    elif second == 3 and first in (2, 3):
        found += [((first, 2), 1, -1)]
    if half == 0:
        return [(SLOT_OF[p], axis, way) for p, axis, way in found]
    return [(SLOT_OF[p[::-1]], 1 - axis, way) for p, axis, way in found]


def choose(index, low, high, work):
    if high - low == 1:
        work(low)
        return
    middle = (low + high) // 2
    pl.when(index < middle)(lambda: choose(index, low, middle, work))
    pl.when(index >= middle)(lambda: choose(index, middle, high, work))


def kernel(
    emb_hbm, cent_hbm, out_hbm, count_out, log_out,
    rows, probs, cent, emb, own_sum, sum_send, sum_recv, final,
    part_src, part_dst, inv, inv_src, inv_row, count, count_src, count_dst, count_all, sq_src, sq_dst,
    load_sem, row_send, row_recv, sib_send, sib_recv, pre_send, pre_recv, late_send, late_recv,
    part_send, part_recv, inv_send, inv_recv,
    sum_ssem, sum_rsem, cnt_send, cnt_recv, sq_send, sq_recv, out_sem, out_send, out_recv, all_send, all_recv,
):
    dp = lax.axis_index("dp")
    comp = lax.axis_index("comp")
    core = lax.rem(dp, 2)
    other = 1 - core
    x_lo = dp // 2
    y = lax.rem(comp, 4)
    x = lax.rem(comp // 4, 2) * 2 + x_lo
    z = comp // 8
    sign = 1 - 2 * core

    at_y = [lax.rem(y + sign * d + 4, 4) for d in range(4)]
    at_z = [lax.rem(z + sign * d + 4, 4) * 8 for d in range(4)]
    at_x = [lax.rem(x + d, 4) for d in range(4)]
    at_x_comp = [(place // 2) * 4 for place in at_x]
    at_x_dp = [lax.rem(place, 2) * 2 for place in at_x]
    cores = (core, other)

    def device(dx, dy, dz, dcore):
        comp_id = at_z[dz % 4] + at_x_comp[dx % 4] + at_y[dy % 4]
        return {"dp": at_x_dp[dx % 4] + cores[dcore], "comp": comp_id}

    def remote(src, dst, ssem, rsem, target):
        return pltpu.make_async_remote_copy(
            src_ref=src, dst_ref=dst, send_sem=ssem, recv_sem=rsem, device_id=target, device_id_type=MESH
        )

    def wait_bytes(ref, sem):
        pltpu.make_async_copy(ref, ref, sem).wait()

    sibling = device(0, 0, 0, 1)
    x_far = device(2, 0, 0, 0)
    x_pair = {"dp": (1 - x_lo) * 2 + core, "comp": comp}

    barrier = pltpu.get_barrier_semaphore()
    greeted = 0
    for dy, dz in ORDER:
        for dcore in (0, 1):
            if (dy, dz, dcore) != (0, 0, 0):
                pl.semaphore_signal(barrier, inc=1, device_id=device(0, dy, dz, dcore), device_id_type=MESH)
                greeted += 1
            pl.semaphore_signal(barrier, inc=1, device_id=device(2, dy, dz, dcore), device_id_type=MESH)
            greeted += 1
    for dx in (1, 3):
        pl.semaphore_signal(barrier, inc=1, device_id=device(dx, 0, 0, 0), device_id_type=MESH)
        greeted += 1

    emb_copy = pltpu.make_async_copy(emb_hbm, emb, load_sem.at[0])
    emb_copy.start()
    cent_copy = pltpu.make_async_copy(cent_hbm.at[pl.ds(core * 1024, 1024)], cent, load_sem.at[1])
    cent_copy.start()

    def unit(values):
        floats = values.astype(F32)
        return (floats * lax.rsqrt(jnp.sum(floats * floats, axis=1, keepdims=True) + 1e-06)).astype(BF16)

    emb_copy.wait()
    rows[pl.ds(0, OWN), :] = unit(emb[...])
    pl.semaphore_wait(barrier, greeted)

    pre = remote(rows.at[pl.ds(0, EARLY)], rows.at[pl.ds(OWN, EARLY)], pre_send, pre_recv, x_far)
    pre.start()

    def row_copy(slot, half, child, axis, way):
        dy, dz = (way, 0) if axis == 0 else (0, way)
        return remote(
            rows.at[pl.ds(slot * STEP + half * HALF, HALF)],
            rows.at[pl.ds(child * STEP + half * HALF, HALF)],
            row_send,
            row_recv.at[child, half],
            device(0, dy, dz, 0),
        )

    def hand_on(slot, half):
        for child, axis, way in children(slot, half):
            row_copy(slot, half, child, axis, way).start()

    def late_copy(slot):
        at = slot * STEP
        return remote(
            rows.at[pl.ds(at + EARLY, OWN - EARLY)],
            rows.at[pl.ds(at + OWN + EARLY, OWN - EARLY)],
            late_send,
            late_recv.at[slot],
            x_far,
        )

    def to_sibling(slot, late):
        first, size = (OWN + EARLY, OWN - EARLY) if late else (0, OWN + EARLY)
        at = slot * STEP + first
        return remote(
            rows.at[pl.ds(at, size)], rows.at[pl.ds(at + NODE, size)], sib_send, sib_recv.at[slot, late], sibling
        )

    def arrive(slot):
        for half in (0, 1):
            row_copy(slot, half, slot, 0, 1).wait_recv()
            hand_on(slot, half)
        late_copy(slot).start()
        to_sibling(slot, 0).start()

    hand_on(0, 0)
    pre.wait_recv()
    hand_on(0, 1)
    late_copy(0).start()
    to_sibling(0, 0).start()

    cent_copy.wait()

    def unit_block(i, carry):
        block = pl.ds(i * 128, 128)
        cent[block, :] = unit(cent[block, :])
        return carry

    lax.fori_loop(0, 8, unit_block, 0)
    def score(slot):
        at = pl.ds((slot - 1) * STEP, 2 * STEP)
        scores = lax.dot_general(cent[...], rows[at, :], (((1,), (1,)), ((), ())), preferred_element_type=F32)
        p = jnp.exp(scores * 10.0 - 10.0)
        probs[:, at] = p.astype(BF16)
        part = jnp.sum(p, axis=0, keepdims=True)
        for i in (0, 1):
            node = part[:, i * STEP : (i + 1) * STEP]
            part_src[2 * (slot - 1 + i)] = node[:, :PART]
            part_src[2 * (slot - 1 + i) + 1] = pltpu.roll(node, STEP - NODE, 1)[:, :PART]

    def send_part(slot):
        dy, dz = ORDER[slot]
        for dcore, way in ((0, -1), (1, 1)):
            tile = 2 * slot + dcore
            for dx, first in ((0, 0), (2, 2 * SLOTS)):
                if dx + tile == 0:
                    part_dst[0] = part_src[0]
                else:
                    remote(
                        part_src.at[tile], part_dst.at[first + tile], part_send, part_recv,
                        device(dx, way * dy, way * dz, dcore),
                    ).start()

    def totals_first():
        wait_bytes(part_dst.at[pl.ds(1, 4 * SLOTS - 1)], part_recv)
        near = jnp.sum(part_dst[pl.ds(0, 2 * SLOTS)], axis=0)
        far = jnp.sum(part_dst[pl.ds(2 * SLOTS, 2 * SLOTS)], axis=0)
        lane = lax.broadcasted_iota(jnp.int32, (1, PART), 1)
        total = near + jnp.where(lane < OWN, pltpu.roll(far, PART - OWN, 1), pltpu.roll(far, OWN, 1))
        total = jnp.where(lane < NODE, total, 1.0)
        inv_src[...] = 1.0 / total
        inv[0] = 1.0 / total
        for slot, (dy, dz) in enumerate(ORDER):
            for dcore in (0, 1):
                if slot + dcore > 0:
                    remote(
                        inv_src, inv.at[2 * slot + dcore], inv_send, inv_recv, device(0, dy, dz, dcore)
                    ).start()
        log_out[...] = jnp.log(total[:, :128]) + 10.0

    def totals_second():
        wait_bytes(inv.at[pl.ds(1, 2 * SLOTS - 1)], inv_recv)
        lane = lax.broadcasted_iota(jnp.int32, (1, STEP), 1)
        rest = jnp.zeros((1, STEP - PART), F32)
        for slot in range(SLOTS):
            mine = jnp.concatenate([inv[2 * slot], rest], axis=1)
            theirs = pltpu.roll(jnp.concatenate([inv[2 * slot + 1], rest], axis=1), NODE, 1)
            inv_row[:, pl.ds(slot * STEP, STEP)] = jnp.where(lane < NODE, mine, theirs)

    def scale(start, size):
        def block(i, carry):
            at = pl.ds(start + i * 64, 64)
            total = jnp.zeros((64, 128), F32)
            for tile in range(ROWS // 128):
                lanes = pl.ds(tile * 128, 128)
                weights = (probs[at, lanes].astype(F32) * inv_row[:, lanes]).astype(BF16)
                probs[at, lanes] = weights
                total = total + weights.astype(F32)
            count[at, :] = total
            return carry

        lax.fori_loop(0, size // 64, block, 0)

    def to_row(block):
        return jnp.sum(block.T, axis=0, keepdims=True)

    def weighted(start, column):
        return lax.dot_general(
            probs[pl.ds(start, LUMP), :],
            rows[:, pl.ds(column, 512)],
            (((1,), (0,)), ((), ())),
            preferred_element_type=F32,
        )

    def sum_copy(m):
        at = pl.ds(m * LUMP, LUMP)
        return remote(sum_send.at[at], sum_recv.at[at], sum_ssem.at[m], sum_rsem.at[m], x_pair)

    count_copy = remote(count_src, count_dst, cnt_send, cnt_recv, x_pair)

    def step(t, carry):
        @pl.when(t < SLOTS - LEAD)
        def _():
            choose(t + LEAD, LEAD, SLOTS, arrive)

        late_copy(t).wait_recv()
        to_sibling(t, 1).start()

        @pl.when(lax.rem(t, 2) == 1)
        def _():
            for slot in (t - 1, t):
                for late in (0, 1):
                    to_sibling(slot, late).wait_recv()
            score(t)
            choose(t // 2, 0, SLOTS // 2, lambda k: (send_part(2 * k), send_part(2 * k + 1)))

        return carry

    for slot in range(1, LEAD):
        arrive(slot)
    lax.fori_loop(0, SLOTS, step, 0)
    totals_first()
    totals_second()

    def partner_half(m, carry):
        scale(m * LUMP, LUMP)
        sum_send[pl.ds(m * LUMP, LUMP), :] = weighted(m * LUMP, (1 - x_lo) * 512).astype(BF16)
        sum_copy(m).start()
        return carry

    lax.fori_loop(0, LUMPS, partner_half, 0)

    for r in range(8):
        count_src[r : r + 1, :] = to_row(count[pl.ds(r * 128, 128), :])
    count_copy.start()

    def own_half(m, carry):
        own_sum[pl.ds(m * LUMP, LUMP), :] = weighted(m * LUMP, x_lo * 512)
        return carry

    lax.fori_loop(0, LUMPS, own_half, 0)

    def sq_copy(m):
        return remote(sq_src.at[m], sq_dst.at[m], sq_send.at[m], sq_recv.at[m], x_pair)

    def out_copies(m):
        at = pl.ds(m * LUMP, LUMP)
        place = pl.ds(core * 1024 + m * LUMP, LUMP)
        local = pltpu.make_async_copy(
            final.at[at, pl.ds(pl.multiple_of(core * 256, 256), 256)], out_hbm.at[place], out_sem.at[m]
        )
        away = remote(
            final.at[at, pl.ds(pl.multiple_of(other * 256, 256), 256)],
            out_hbm.at[place],
            out_send.at[m],
            out_recv.at[m],
            sibling,
        )
        return local, away

    def finish(m):
        at = pl.ds(m * LUMP, LUMP)
        sum_copy(m).wait_recv()
        total = own_sum[at, :] + sum_recv[at, :].astype(F32)
        own_sum[at, :] = total
        squares = total * total
        lanes = squares[:, :128] + squares[:, 128:256] + squares[:, 256:384] + squares[:, 384:]
        sq_src[m] = jnp.concatenate(
            [to_row(lanes[i * 128 : (i + 1) * 128]) for i in range(LUMP // 128)]
            + [jnp.zeros((8 - LUMP // 128, 128), F32)],
            axis=0,
        )
        sq_copy(m).start()

    def normalize(m):
        sq_copy(m).wait_recv()
        for i in range(LUMP // 128):
            at = pl.ds(m * LUMP + i * 128, 128)
            squares = sq_src[m, i : i + 1, :] + sq_dst[m, i : i + 1, :]
            factor = jnp.broadcast_to(lax.rsqrt(squares + 1e-06), (128, 128)).T
            for tile in range(4):
                lanes = pl.ds(tile * 128, 128)
                final[at, lanes] = (own_sum[at, lanes] * factor).astype(BF16)
        local, away = out_copies(m)
        local.start()
        away.start()

    def last(m, carry):
        pl.when(m < LUMPS)(lambda: finish(m))
        pl.when(m > 0)(lambda: normalize(m - 1))
        return carry

    lax.fori_loop(0, LUMPS + 1, last, 0)

    count_copy.wait_recv()
    mine = pl.ds(pl.multiple_of(core * 8, 8), 8)
    count_all[mine, :] = count_src[...] + count_dst[...]
    all_copy = remote(count_all.at[mine], count_all.at[mine], all_send, all_recv, sibling)
    all_copy.start()

    pre.wait_send()
    wait_bytes(rows.at[pl.ds(0, (SLOTS - 1) * 2 * HALF)], row_send)
    wait_bytes(rows.at[pl.ds(0, SLOTS * NODE)], sib_send)
    wait_bytes(rows.at[pl.ds(0, SLOTS * (OWN - EARLY))], late_send)
    wait_bytes(part_dst.at[pl.ds(1, 4 * SLOTS - 1)], part_send)
    wait_bytes(inv.at[pl.ds(1, 2 * SLOTS - 1)], inv_send)
    count_copy.wait_send()
    for m in range(LUMPS):
        sum_copy(m).wait_send()
        sq_copy(m).wait_send()
        local, away = out_copies(m)
        local.wait()
        away.wait()
    all_copy.wait()
    count_out[...] = count_all[...]


def place_results(new_ref, count_ref, log_ref, new_out, count_out, log_out):
    new_out[...] = new_ref[...]
    count_out[...] = count_ref[...]
    log_out[...] = log_ref[:, :OWN]


def on_device(embeddings, centroids):
    dma = pltpu.SemaphoreType.DMA
    any_space = pl.BlockSpec(memory_space=pl.ANY)
    vmem = pl.BlockSpec(memory_space=pltpu.VMEM)
    quarter = pl.BlockSpec((512, 256), lambda i: (i, 0))

    def whole(*shape):
        return pl.BlockSpec(shape, lambda i: (0, 0))

    new_centroids, counts, logs = pl.pallas_call(
        kernel,
        out_shape=(
            jax.ShapeDtypeStruct((2048, 256), BF16),
            jax.ShapeDtypeStruct((16, 128), F32),
            jax.ShapeDtypeStruct((1, 128), F32),
        ),
        in_specs=[any_space, any_space],
        out_specs=(any_space, vmem, vmem),
        scratch_shapes=[
            pltpu.VMEM((ROWS, 1024), BF16),
            pltpu.VMEM((1024, ROWS), BF16),
            pltpu.VMEM((1024, 1024), BF16),
            pltpu.VMEM((OWN, 1024), BF16),
            pltpu.VMEM((1024, 512), F32),
            pltpu.VMEM((1024, 512), BF16),
            pltpu.VMEM((1024, 512), BF16),
            pltpu.VMEM((1024, 512), BF16),
            pltpu.VMEM((2 * SLOTS, 1, PART), F32),
            pltpu.VMEM((4 * SLOTS, 1, PART), F32),
            pltpu.VMEM((2 * SLOTS, 1, PART), F32),
            pltpu.VMEM((1, PART), F32),
            pltpu.VMEM((1, ROWS), F32),
            pltpu.VMEM((1024, 128), F32),
            pltpu.VMEM((8, 128), F32),
            pltpu.VMEM((8, 128), F32),
            pltpu.VMEM((16, 128), F32),
            pltpu.VMEM((LUMPS, 8, 128), F32),
            pltpu.VMEM((LUMPS, 8, 128), F32),
            dma((2,)),
            dma, dma((SLOTS, 2)),
            dma, dma((SLOTS, 2)),
            dma, dma,
            dma, dma((SLOTS,)),
            dma, dma,
            dma, dma,
            dma((LUMPS,)), dma((LUMPS,)),
            dma, dma,
            dma((LUMPS,)), dma((LUMPS,)),
            dma((LUMPS,)), dma((LUMPS,)), dma((LUMPS,)),
            dma, dma,
        ],
        compiler_params=pltpu.CompilerParams(
            collective_id=0, has_side_effects=True, vmem_limit_bytes=60 * 1024 * 1024
        ),
        name="soft_kmeans",
    )(embeddings, centroids)
    new_centroids, counts, logs = pl.pallas_call(
        place_results,
        out_shape=(
            jax.ShapeDtypeStruct((2048, 256), BF16),
            jax.ShapeDtypeStruct((16, 128), F32),
            jax.ShapeDtypeStruct((1, OWN), F32),
        ),
        grid=(4,),
        in_specs=[quarter, whole(16, 128), whole(1, 128)],
        out_specs=(quarter, whole(16, 128), whole(1, OWN)),
        name="place_results",
    )(new_centroids, counts, logs)
    return new_centroids, counts.reshape(2048), logs.reshape(OWN)


def solution(mesh):
    return jax.shard_map(
        on_device,
        mesh=mesh,
        in_specs=(P(("dp", "comp"), None), P("comp", None)),
        out_specs=(P("comp", "dp"), P("comp"), P(("dp", "comp"))),
        check_vma=False,
    )
```

```python
import jax
import jax.numpy as jnp
from jax import lax
from jax.experimental import pallas as pl
from jax.experimental.pallas import tpu as pltpu
from jax.sharding import PartitionSpec as P

MESH = pl.DeviceIdType.MESH
F32 = jnp.float32
BF16 = jnp.bfloat16

ORDER = (
    (0, 0), (1, 0), (0, 1), (3, 0), (0, 3), (2, 0), (0, 2), (1, 1),
    (3, 3), (1, 3), (3, 1), (2, 1), (1, 2), (2, 3), (3, 2), (2, 2),
)
SLOTS = len(ORDER)
SLOT_OF = {place: slot for slot, place in enumerate(ORDER)}
OWN = 96
EARLY = 64
NODE = 2 * OWN
HALVES = ((0, OWN), (OWN, EARLY))
STEP = 2 * NODE
ROWS = SLOTS * STEP
LEAD = 3
PART = 256
LUMP = 256
LUMPS = 1024 // LUMP


def children(slot, half):
    place = ORDER[slot]
    first, second = place if half == 0 else place[::-1]
    found = []
    if second == 0:
        if first == 0:
            found += [((1, 0), 0, 1), ((3, 0), 0, -1)]
        if first == 1:
            found += [((2, 0), 0, 1)]
        found += [((first, 1), 1, 1), ((first, 3), 1, -1)]
    elif second == 1 and first in (0, 1):
        found += [((first, 2), 1, 1)]
    elif second == 3 and first in (2, 3):
        found += [((first, 2), 1, -1)]
    if half == 0:
        return [(SLOT_OF[p], axis, way) for p, axis, way in found]
    return [(SLOT_OF[p[::-1]], 1 - axis, way) for p, axis, way in found]


def choose(index, low, high, work):
    if high - low == 1:
        work(low)
        return
    middle = (low + high) // 2
    pl.when(index < middle)(lambda: choose(index, low, middle, work))
    pl.when(index >= middle)(lambda: choose(index, middle, high, work))


def kernel(
    emb_hbm, cent_hbm, out_hbm, count_out, log_out,
    rows, probs, cent, emb, own_sum, sum_send, sum_recv, final,
    part_src, part_dst, inv, inv_src, inv_row, count, count_src, count_dst, count_all, sq_src, sq_dst,
    load_sem, row_send, row_recv, sib_send, sib_recv, pre_send, pre_recv, late_send, late_recv,
    part_send, part_recv, inv_send, inv_recv,
    sum_ssem, sum_rsem, cnt_send, cnt_recv, sq_send, sq_recv, out_sem, out_send, out_recv, all_send, all_recv,
):
    dp = lax.axis_index("dp")
    comp = lax.axis_index("comp")
    core = lax.rem(dp, 2)
    other = 1 - core
    x_lo = dp // 2
    y = lax.rem(comp, 4)
    x = lax.rem(comp // 4, 2) * 2 + x_lo
    z = comp // 8
    sign = 1 - 2 * core

    at_y = [lax.rem(y + sign * d + 4, 4) for d in range(4)]
    at_z = [lax.rem(z + sign * d + 4, 4) * 8 for d in range(4)]
    at_first = [y_id * other + z_id * core for y_id, z_id in zip(at_y, at_z)]
    at_second = [y_id * core + z_id * other for y_id, z_id in zip(at_y, at_z)]
    at_x = [lax.rem(x + d, 4) for d in range(4)]
    at_x_comp = [(place // 2) * 4 for place in at_x]
    at_x_dp = [lax.rem(place, 2) * 2 for place in at_x]
    cores = (core, other)

    def device(dx, first, second, dcore):
        comp_id = at_first[first % 4] + at_x_comp[dx % 4] + at_second[second % 4]
        return {"dp": at_x_dp[dx % 4] + cores[dcore], "comp": comp_id}

    def remote(src, dst, ssem, rsem, target):
        return pltpu.make_async_remote_copy(
            src_ref=src, dst_ref=dst, send_sem=ssem, recv_sem=rsem, device_id=target, device_id_type=MESH
        )

    def wait_bytes(ref, sem):
        pltpu.make_async_copy(ref, ref, sem).wait()

    sibling = device(0, 0, 0, 1)
    x_far = device(2, 0, 0, 0)
    x_pair = {"dp": (1 - x_lo) * 2 + core, "comp": comp}

    emb_copy = pltpu.make_async_copy(emb_hbm, emb, load_sem.at[0])
    emb_copy.start()
    cent_copy = pltpu.make_async_copy(cent_hbm.at[pl.ds(core * 1024, 1024)], cent, load_sem.at[1])
    cent_copy.start()

    barrier = pltpu.get_barrier_semaphore()
    greeted = 0
    for place in ORDER:
        for dcore in (0, 1):
            if (*place, dcore) != (0, 0, 0):
                pl.semaphore_signal(barrier, inc=1, device_id=device(0, *place, dcore), device_id_type=MESH)
                greeted += 1
            pl.semaphore_signal(barrier, inc=1, device_id=device(2, *place, dcore), device_id_type=MESH)
            greeted += 1
    for dx in (1, 3):
        pl.semaphore_signal(barrier, inc=1, device_id=device(dx, 0, 0, 0), device_id_type=MESH)
        greeted += 1

    def unit(values):
        floats = values.astype(F32)
        return (floats * lax.rsqrt(jnp.sum(floats * floats, axis=1, keepdims=True) + 1e-06)).astype(BF16)

    emb_copy.wait()
    rows[pl.ds(0, OWN), :] = unit(emb[...])
    pl.semaphore_wait(barrier, greeted)

    pre = remote(rows.at[pl.ds(0, EARLY)], rows.at[pl.ds(OWN, EARLY)], pre_send, pre_recv, x_far)
    pre.start()

    def row_copy(slot, half, child, axis, way):
        first, second = (way, 0) if axis == 0 else (0, way)
        start, size = HALVES[half]
        return remote(
            rows.at[pl.ds(slot * STEP + start, size)],
            rows.at[pl.ds(child * STEP + start, size)],
            row_send,
            row_recv.at[child, half],
            device(0, first, second, 0),
        )

    def hand_on(slot, half):
        for child, axis, way in children(slot, half):
            row_copy(slot, half, child, axis, way).start()

    def late_copy(slot):
        at = slot * STEP
        return remote(
            rows.at[pl.ds(at + EARLY, OWN - EARLY)],
            rows.at[pl.ds(at + OWN + EARLY, OWN - EARLY)],
            late_send,
            late_recv.at[slot],
            x_far,
        )

    def to_sibling(slot, late):
        first, size = (OWN + EARLY, OWN - EARLY) if late else (0, OWN + EARLY)
        at = slot * STEP + first
        return remote(
            rows.at[pl.ds(at, size)], rows.at[pl.ds(at + NODE, size)], sib_send, sib_recv.at[slot, late], sibling
        )

    def arrive(slot):
        row_copy(slot, 0, slot, 0, 1).wait_recv()
        hand_on(slot, 0)
        late_copy(slot).start()
        row_copy(slot, 1, slot, 0, 1).wait_recv()
        hand_on(slot, 1)
        to_sibling(slot, 0).start()

    hand_on(0, 0)
    pre.wait_recv()
    hand_on(0, 1)
    late_copy(0).start()
    to_sibling(0, 0).start()

    cent_copy.wait()

    def unit_block(i, carry):
        block = pl.ds(i * 128, 128)
        cent[block, :] = unit(cent[block, :])
        return carry

    lax.fori_loop(0, 8, unit_block, 0)
    def score(slot):
        at = pl.ds((slot - 1) * STEP, 2 * STEP)
        scores = lax.dot_general(cent[...], rows[at, :], (((1,), (1,)), ((), ())), preferred_element_type=F32)
        p = jnp.exp(scores * 10.0 - 10.0)
        probs[:, at] = p.astype(BF16)
        part = jnp.sum(p, axis=0, keepdims=True)
        for i in (0, 1):
            node = part[:, i * STEP : (i + 1) * STEP]
            part_src[2 * (slot - 1 + i)] = node[:, :PART]
            part_src[2 * (slot - 1 + i) + 1] = pltpu.roll(node, STEP - NODE, 1)[:, :PART]

    def send_part(slot):
        first, second = ORDER[slot]
        for dcore, place in ((0, (-first, -second)), (1, (second, first))):
            tile = 2 * slot + dcore
            for dx, base in ((0, 0), (2, 2 * SLOTS)):
                if dx + tile == 0:
                    part_dst[0] = part_src[0]
                else:
                    remote(
                        part_src.at[tile], part_dst.at[base + tile], part_send, part_recv, device(dx, *place, dcore)
                    ).start()

    def totals_first():
        wait_bytes(part_dst.at[pl.ds(1, 4 * SLOTS - 1)], part_recv)
        near = jnp.sum(part_dst[pl.ds(0, 2 * SLOTS)], axis=0)
        far = jnp.sum(part_dst[pl.ds(2 * SLOTS, 2 * SLOTS)], axis=0)
        lane = lax.broadcasted_iota(jnp.int32, (1, PART), 1)
        total = near + jnp.where(lane < OWN, pltpu.roll(far, PART - OWN, 1), pltpu.roll(far, OWN, 1))
        total = jnp.where(lane < NODE, total, 1.0)
        inv_src[...] = 1.0 / total
        inv[0] = 1.0 / total
        for slot, place in enumerate(ORDER):
            for dcore in (0, 1):
                if slot + dcore > 0:
                    remote(
                        inv_src, inv.at[2 * slot + dcore], inv_send, inv_recv, device(0, *place, dcore)
                    ).start()
        log_out[...] = jnp.log(total[:, :128]) + 10.0

    def totals_second():
        wait_bytes(inv.at[pl.ds(1, 2 * SLOTS - 1)], inv_recv)
        lane = lax.broadcasted_iota(jnp.int32, (1, STEP), 1)
        rest = jnp.zeros((1, STEP - PART), F32)
        for slot in range(SLOTS):
            mine = jnp.concatenate([inv[2 * slot], rest], axis=1)
            theirs = pltpu.roll(jnp.concatenate([inv[2 * slot + 1], rest], axis=1), NODE, 1)
            inv_row[:, pl.ds(slot * STEP, STEP)] = jnp.where(lane < NODE, mine, theirs)

    def scale(start, size):
        def block(i, carry):
            at = pl.ds(start + i * 64, 64)
            total = jnp.zeros((64, 128), F32)
            for tile in range(ROWS // 128):
                lanes = pl.ds(tile * 128, 128)
                weights = (probs[at, lanes].astype(F32) * inv_row[:, lanes]).astype(BF16)
                probs[at, lanes] = weights
                total = total + weights.astype(F32)
            count[at, :] = total
            return carry

        lax.fori_loop(0, size // 64, block, 0)

    def to_row(block):
        return jnp.sum(block.T, axis=0, keepdims=True)

    def weighted(start, column):
        return lax.dot_general(
            probs[pl.ds(start, LUMP), :],
            rows[:, pl.ds(column, 512)],
            (((1,), (0,)), ((), ())),
            preferred_element_type=F32,
        )

    def sum_copy(m):
        at = pl.ds(m * LUMP, LUMP)
        return remote(sum_send.at[at], sum_recv.at[at], sum_ssem.at[m], sum_rsem.at[m], x_pair)

    count_copy = remote(count_src, count_dst, cnt_send, cnt_recv, x_pair)

    def step(t, carry):
        @pl.when(t < SLOTS - LEAD)
        def _():
            choose(t + LEAD, LEAD, SLOTS, arrive)

        late_copy(t).wait_recv()
        to_sibling(t, 1).start()

        @pl.when(lax.rem(t, 2) == 1)
        def _():
            for slot in (t - 1, t):
                for late in (0, 1):
                    to_sibling(slot, late).wait_recv()
            score(t)
            choose(t // 2, 0, SLOTS // 2, lambda k: (send_part(2 * k), send_part(2 * k + 1)))

        return carry

    for slot in range(1, LEAD):
        arrive(slot)
    lax.fori_loop(0, SLOTS, step, 0)
    totals_first()
    totals_second()

    def partner_half(m, carry):
        scale(m * LUMP, LUMP)
        sum_send[pl.ds(m * LUMP, LUMP), :] = weighted(m * LUMP, (1 - x_lo) * 512).astype(BF16)
        sum_copy(m).start()
        return carry

    lax.fori_loop(0, LUMPS, partner_half, 0)

    for r in range(8):
        count_src[r : r + 1, :] = to_row(count[pl.ds(r * 128, 128), :])
    count_copy.start()

    def own_half(m, carry):
        own_sum[pl.ds(m * LUMP, LUMP), :] = weighted(m * LUMP, x_lo * 512)
        return carry

    lax.fori_loop(0, LUMPS, own_half, 0)

    def sq_copy(m):
        return remote(sq_src.at[m], sq_dst.at[m], sq_send.at[m], sq_recv.at[m], x_pair)

    def out_copies(m):
        at = pl.ds(m * LUMP, LUMP)
        place = pl.ds(core * 1024 + m * LUMP, LUMP)
        local = pltpu.make_async_copy(
            final.at[at, pl.ds(pl.multiple_of(core * 256, 256), 256)], out_hbm.at[place], out_sem.at[m]
        )
        away = remote(
            final.at[at, pl.ds(pl.multiple_of(other * 256, 256), 256)],
            out_hbm.at[place],
            out_send.at[m],
            out_recv.at[m],
            sibling,
        )
        return local, away

    def finish(m):
        at = pl.ds(m * LUMP, LUMP)
        sum_copy(m).wait_recv()
        total = own_sum[at, :] + sum_recv[at, :].astype(F32)
        own_sum[at, :] = total
        squares = total * total
        lanes = squares[:, :128] + squares[:, 128:256] + squares[:, 256:384] + squares[:, 384:]
        sq_src[m] = jnp.concatenate(
            [to_row(lanes[i * 128 : (i + 1) * 128]) for i in range(LUMP // 128)]
            + [jnp.zeros((8 - LUMP // 128, 128), F32)],
            axis=0,
        )
        sq_copy(m).start()

    def normalize(m):
        sq_copy(m).wait_recv()
        for i in range(LUMP // 128):
            at = pl.ds(m * LUMP + i * 128, 128)
            squares = sq_src[m, i : i + 1, :] + sq_dst[m, i : i + 1, :]
            factor = jnp.broadcast_to(lax.rsqrt(squares + 1e-06), (128, 128)).T
            for tile in range(4):
                lanes = pl.ds(tile * 128, 128)
                final[at, lanes] = (own_sum[at, lanes] * factor).astype(BF16)
        local, away = out_copies(m)
        local.start()
        away.start()

    def last(m, carry):
        pl.when(m < LUMPS)(lambda: finish(m))
        pl.when(m > 0)(lambda: normalize(m - 1))
        return carry

    lax.fori_loop(0, LUMPS + 1, last, 0)

    count_copy.wait_recv()
    mine = pl.ds(pl.multiple_of(core * 8, 8), 8)
    count_all[mine, :] = count_src[...] + count_dst[...]
    all_copy = remote(count_all.at[mine], count_all.at[mine], all_send, all_recv, sibling)
    all_copy.start()

    pre.wait_send()
    wait_bytes(rows.at[pl.ds(0, (SLOTS - 1) * (OWN + EARLY))], row_send)
    wait_bytes(rows.at[pl.ds(0, SLOTS * NODE)], sib_send)
    wait_bytes(rows.at[pl.ds(0, SLOTS * (OWN - EARLY))], late_send)
    wait_bytes(part_dst.at[pl.ds(1, 4 * SLOTS - 1)], part_send)
    wait_bytes(inv.at[pl.ds(1, 2 * SLOTS - 1)], inv_send)
    count_copy.wait_send()
    for m in range(LUMPS):
        sum_copy(m).wait_send()
        sq_copy(m).wait_send()
        local, away = out_copies(m)
        local.wait()
        away.wait()
    all_copy.wait()
    count_out[...] = count_all[...]


def place_results(new_ref, count_ref, log_ref, new_out, count_out, log_out):
    new_out[...] = new_ref[...]
    count_out[...] = count_ref[...]
    log_out[...] = log_ref[:, :OWN]


def on_device(embeddings, centroids):
    dma = pltpu.SemaphoreType.DMA
    any_space = pl.BlockSpec(memory_space=pl.ANY)
    vmem = pl.BlockSpec(memory_space=pltpu.VMEM)
    quarter = pl.BlockSpec((512, 256), lambda i: (i, 0))

    def whole(*shape):
        return pl.BlockSpec(shape, lambda i: (0, 0))

    new_centroids, counts, logs = pl.pallas_call(
        kernel,
        out_shape=(
            jax.ShapeDtypeStruct((2048, 256), BF16),
            jax.ShapeDtypeStruct((16, 128), F32),
            jax.ShapeDtypeStruct((1, 128), F32),
        ),
        in_specs=[any_space, any_space],
        out_specs=(any_space, vmem, vmem),
        scratch_shapes=[
            pltpu.VMEM((ROWS, 1024), BF16),
            pltpu.VMEM((1024, ROWS), BF16),
            pltpu.VMEM((1024, 1024), BF16),
            pltpu.VMEM((OWN, 1024), BF16),
            pltpu.VMEM((1024, 512), F32),
            pltpu.VMEM((1024, 512), BF16),
            pltpu.VMEM((1024, 512), BF16),
            pltpu.VMEM((1024, 512), BF16),
            pltpu.VMEM((2 * SLOTS, 1, PART), F32),
            pltpu.VMEM((4 * SLOTS, 1, PART), F32),
            pltpu.VMEM((2 * SLOTS, 1, PART), F32),
            pltpu.VMEM((1, PART), F32),
            pltpu.VMEM((1, ROWS), F32),
            pltpu.VMEM((1024, 128), F32),
            pltpu.VMEM((8, 128), F32),
            pltpu.VMEM((8, 128), F32),
            pltpu.VMEM((16, 128), F32),
            pltpu.VMEM((LUMPS, 8, 128), F32),
            pltpu.VMEM((LUMPS, 8, 128), F32),
            dma((2,)),
            dma, dma((SLOTS, 2)),
            dma, dma((SLOTS, 2)),
            dma, dma,
            dma, dma((SLOTS,)),
            dma, dma,
            dma, dma,
            dma((LUMPS,)), dma((LUMPS,)),
            dma, dma,
            dma((LUMPS,)), dma((LUMPS,)),
            dma((LUMPS,)), dma((LUMPS,)), dma((LUMPS,)),
            dma, dma,
        ],
        compiler_params=pltpu.CompilerParams(
            collective_id=0, has_side_effects=True, vmem_limit_bytes=60 * 1024 * 1024
        ),
        name="soft_kmeans",
    )(embeddings, centroids)
    new_centroids, counts, logs = pl.pallas_call(
        place_results,
        out_shape=(
            jax.ShapeDtypeStruct((2048, 256), BF16),
            jax.ShapeDtypeStruct((16, 128), F32),
            jax.ShapeDtypeStruct((1, OWN), F32),
        ),
        grid=(4,),
        in_specs=[quarter, whole(16, 128), whole(1, 128)],
        out_specs=(quarter, whole(16, 128), whole(1, OWN)),
        name="place_results",
    )(new_centroids, counts, logs)
    return new_centroids, counts.reshape(2048), logs.reshape(OWN)


def solution(mesh):
    return jax.shard_map(
        on_device,
        mesh=mesh,
        in_specs=(P(("dp", "comp"), None), P("comp", None)),
        out_specs=(P("comp", "dp"), P("comp"), P(("dp", "comp"))),
        check_vma=False,
    )
```

```python
import jax
import jax.numpy as jnp
from jax import lax
from jax.experimental import pallas as pl
from jax.experimental.pallas import tpu as pltpu
from jax.sharding import PartitionSpec as P

MESH = pl.DeviceIdType.MESH
F32 = jnp.float32
BF16 = jnp.bfloat16

ORDER = (
    (0, 0), (1, 0), (0, 1), (3, 0), (0, 3), (2, 0), (0, 2), (1, 1),
    (3, 3), (1, 3), (3, 1), (2, 1), (1, 2), (2, 3), (3, 2), (2, 2),
)
SLOTS = len(ORDER)
SLOT_OF = {place: slot for slot, place in enumerate(ORDER)}
OWN = 96
EARLY = 64
NODE = 2 * OWN
HALVES = ((0, OWN), (OWN, EARLY))
STEP = 2 * NODE
ROWS = SLOTS * STEP
LEAD = 3
PART = 256
LUMP = 256
LUMPS = 1024 // LUMP


def children(slot, half):
    place = ORDER[slot]
    first, second = place if half == 0 else place[::-1]
    found = []
    if second == 0:
        if first == 0:
            found += [((1, 0), 0, 1), ((3, 0), 0, -1)]
        if first == 1:
            found += [((2, 0), 0, 1)]
        found += [((first, 1), 1, 1), ((first, 3), 1, -1)]
    elif second == 1 and first in (0, 1):
        found += [((first, 2), 1, 1)]
    elif second == 3 and first in (2, 3):
        found += [((first, 2), 1, -1)]
    if half == 0:
        return [(SLOT_OF[p], axis, way) for p, axis, way in found]
    return [(SLOT_OF[p[::-1]], 1 - axis, way) for p, axis, way in found]


def choose(index, low, high, work):
    if high - low == 1:
        work(low)
        return
    middle = (low + high) // 2
    pl.when(index < middle)(lambda: choose(index, low, middle, work))
    pl.when(index >= middle)(lambda: choose(index, middle, high, work))


def kernel(
    emb_hbm, cent_hbm, out_hbm, count_out, log_out,
    rows, probs, cent, emb, own_sum, sum_send, sum_recv, final,
    part_src, part_dst, inv, inv_src, inv_row, count, count_src, count_dst, count_all, sq_src, sq_dst,
    load_sem, row_send, row_recv, sib_send, sib_recv, pre_send, pre_recv, late_send, late_recv,
    part_send, part_recv, inv_send, inv_recv,
    sum_ssem, sum_rsem, cnt_send, cnt_recv, sq_send, sq_recv, out_sem, out_send, out_recv, all_send, all_recv,
):
    dp = lax.axis_index("dp")
    comp = lax.axis_index("comp")
    core = lax.rem(dp, 2)
    other = 1 - core
    x_lo = dp // 2
    y = lax.rem(comp, 4)
    x = lax.rem(comp // 4, 2) * 2 + x_lo
    z = comp // 8
    sign = 1 - 2 * core

    at_y = [lax.rem(y + sign * d + 4, 4) for d in range(4)]
    at_z = [lax.rem(z + sign * d + 4, 4) * 8 for d in range(4)]
    at_first = [y_id * other + z_id * core for y_id, z_id in zip(at_y, at_z)]
    at_second = [y_id * core + z_id * other for y_id, z_id in zip(at_y, at_z)]
    at_x = [lax.rem(x + d, 4) for d in range(4)]
    at_x_comp = [(place // 2) * 4 for place in at_x]
    at_x_dp = [lax.rem(place, 2) * 2 for place in at_x]
    cores = (core, other)

    def device(dx, first, second, dcore):
        comp_id = at_first[first % 4] + at_x_comp[dx % 4] + at_second[second % 4]
        return {"dp": at_x_dp[dx % 4] + cores[dcore], "comp": comp_id}

    def remote(src, dst, ssem, rsem, target):
        return pltpu.make_async_remote_copy(
            src_ref=src, dst_ref=dst, send_sem=ssem, recv_sem=rsem, device_id=target, device_id_type=MESH
        )

    def wait_bytes(ref, sem):
        pltpu.make_async_copy(ref, ref, sem).wait()

    sibling = device(0, 0, 0, 1)
    x_far = device(2, 0, 0, 0)
    x_pair = {"dp": (1 - x_lo) * 2 + core, "comp": comp}

    emb_copy = pltpu.make_async_copy(emb_hbm, emb, load_sem.at[0])
    emb_copy.start()
    cent_copy = pltpu.make_async_copy(cent_hbm.at[pl.ds(core * 1024, 1024)], cent, load_sem.at[1])
    cent_copy.start()

    barrier = pltpu.get_barrier_semaphore()
    greeted = 0
    for place in ORDER:
        for dcore in (0, 1):
            if (*place, dcore) != (0, 0, 0):
                pl.semaphore_signal(barrier, inc=1, device_id=device(0, *place, dcore), device_id_type=MESH)
                greeted += 1
            pl.semaphore_signal(barrier, inc=1, device_id=device(2, *place, dcore), device_id_type=MESH)
            greeted += 1
    for dx in (1, 3):
        pl.semaphore_signal(barrier, inc=1, device_id=device(dx, 0, 0, 0), device_id_type=MESH)
        greeted += 1

    def unit(values):
        floats = values.astype(F32)
        return (floats * lax.rsqrt(jnp.sum(floats * floats, axis=1, keepdims=True) + 1e-06)).astype(BF16)

    emb_copy.wait()
    rows[pl.ds(0, OWN), :] = unit(emb[...])
    pl.semaphore_wait(barrier, greeted)

    pre = remote(rows.at[pl.ds(0, EARLY)], rows.at[pl.ds(OWN, EARLY)], pre_send, pre_recv, x_far)
    pre.start()

    def row_copy(slot, half, child, axis, way):
        first, second = (way, 0) if axis == 0 else (0, way)
        start, size = HALVES[half]
        return remote(
            rows.at[pl.ds(slot * STEP + start, size)],
            rows.at[pl.ds(child * STEP + start, size)],
            row_send,
            row_recv.at[child, half],
            device(0, first, second, 0),
        )

    def hand_on(slot, half):
        for child, axis, way in children(slot, half):
            row_copy(slot, half, child, axis, way).start()

    def late_copy(slot):
        at = slot * STEP
        return remote(
            rows.at[pl.ds(at + EARLY, OWN - EARLY)],
            rows.at[pl.ds(at + OWN + EARLY, OWN - EARLY)],
            late_send,
            late_recv.at[slot],
            x_far,
        )

    def to_sibling(slot, late):
        first, size = (OWN + EARLY, OWN - EARLY) if late else (0, OWN + EARLY)
        at = slot * STEP + first
        return remote(
            rows.at[pl.ds(at, size)], rows.at[pl.ds(at + NODE, size)], sib_send, sib_recv.at[slot, late], sibling
        )

    def arrive(slot):
        row_copy(slot, 0, slot, 0, 1).wait_recv()
        hand_on(slot, 0)
        late_copy(slot).start()
        row_copy(slot, 1, slot, 0, 1).wait_recv()
        hand_on(slot, 1)
        to_sibling(slot, 0).start()

    def arrive_late(slot):
        late_copy(slot).wait_recv()
        to_sibling(slot, 1).start()

    hand_on(0, 0)
    pre.wait_recv()
    hand_on(0, 1)
    late_copy(0).start()
    to_sibling(0, 0).start()

    cent_copy.wait()

    def unit_block(i, carry):
        block = pl.ds(i * 128, 128)
        cent[block, :] = unit(cent[block, :])
        return carry

    lax.fori_loop(0, 8, unit_block, 0)
    def score(slot):
        at = pl.ds((slot - 1) * STEP, 2 * STEP)
        scores = lax.dot_general(cent[...], rows[at, :], (((1,), (1,)), ((), ())), preferred_element_type=F32)
        p = jnp.exp(scores * 10.0 - 10.0)
        probs[:, at] = p.astype(BF16)
        part = jnp.sum(p, axis=0, keepdims=True)
        for i in (0, 1):
            node = part[:, i * STEP : (i + 1) * STEP]
            part_src[2 * (slot - 1 + i)] = node[:, :PART]
            part_src[2 * (slot - 1 + i) + 1] = pltpu.roll(node, STEP - NODE, 1)[:, :PART]

    def send_part(slot):
        first, second = ORDER[slot]
        for dcore, place in ((0, (-first, -second)), (1, (second, first))):
            tile = 2 * slot + dcore
            for dx, base in ((0, 0), (2, 2 * SLOTS)):
                if dx + tile == 0:
                    part_dst[0] = part_src[0]
                else:
                    remote(
                        part_src.at[tile], part_dst.at[base + tile], part_send, part_recv, device(dx, *place, dcore)
                    ).start()

    def totals_first():
        wait_bytes(part_dst.at[pl.ds(1, 4 * SLOTS - 1)], part_recv)
        near = jnp.sum(part_dst[pl.ds(0, 2 * SLOTS)], axis=0)
        far = jnp.sum(part_dst[pl.ds(2 * SLOTS, 2 * SLOTS)], axis=0)
        lane = lax.broadcasted_iota(jnp.int32, (1, PART), 1)
        total = near + jnp.where(lane < OWN, pltpu.roll(far, PART - OWN, 1), pltpu.roll(far, OWN, 1))
        total = jnp.where(lane < NODE, total, 1.0)
        inv_src[...] = 1.0 / total
        inv[0] = 1.0 / total
        for slot in reversed(range(SLOTS)):
            place = ORDER[slot]
            for dcore in (0, 1):
                if slot + dcore > 0:
                    remote(
                        inv_src, inv.at[2 * slot + dcore], inv_send, inv_recv, device(0, *place, dcore)
                    ).start()
        log_out[...] = jnp.log(total[:, :128]) + 10.0

    def totals_second():
        wait_bytes(inv.at[pl.ds(1, 2 * SLOTS - 1)], inv_recv)
        lane = lax.broadcasted_iota(jnp.int32, (1, STEP), 1)
        rest = jnp.zeros((1, STEP - PART), F32)
        for slot in range(SLOTS):
            mine = jnp.concatenate([inv[2 * slot], rest], axis=1)
            theirs = pltpu.roll(jnp.concatenate([inv[2 * slot + 1], rest], axis=1), NODE, 1)
            inv_row[:, pl.ds(slot * STEP, STEP)] = jnp.where(lane < NODE, mine, theirs)

    def scale(start, size):
        def block(i, carry):
            at = pl.ds(start + i * 64, 64)
            total = jnp.zeros((64, 128), F32)
            for tile in range(ROWS // 128):
                lanes = pl.ds(tile * 128, 128)
                weights = (probs[at, lanes].astype(F32) * inv_row[:, lanes]).astype(BF16)
                probs[at, lanes] = weights
                total = total + weights.astype(F32)
            count[at, :] = total
            return carry

        lax.fori_loop(0, size // 64, block, 0)

    def to_row(block):
        return jnp.sum(block.T, axis=0, keepdims=True)

    def weighted(start, column):
        return lax.dot_general(
            probs[pl.ds(start, LUMP), :],
            rows[:, pl.ds(column, 512)],
            (((1,), (0,)), ((), ())),
            preferred_element_type=F32,
        )

    def sum_copy(m):
        at = pl.ds(m * LUMP, LUMP)
        return remote(sum_send.at[at], sum_recv.at[at], sum_ssem.at[m], sum_rsem.at[m], x_pair)

    count_copy = remote(count_src, count_dst, cnt_send, cnt_recv, x_pair)

    def step(t, carry):
        @pl.when(t < SLOTS - LEAD)
        def _():
            choose(t + LEAD, LEAD, SLOTS, arrive)

        @pl.when(t < SLOTS - 1)
        def _():
            arrive_late(t + 1)

        @pl.when(lax.rem(t, 2) == 1)
        def _():
            for slot in (t - 1, t):
                for late in (0, 1):
                    to_sibling(slot, late).wait_recv()
            score(t)
            choose(t // 2, 0, SLOTS // 2, lambda k: (send_part(2 * k), send_part(2 * k + 1)))

        return carry

    for slot in range(1, LEAD):
        arrive(slot)
    arrive_late(0)
    lax.fori_loop(0, SLOTS, step, 0)
    totals_first()
    totals_second()

    def partner_half(m, carry):
        scale(m * LUMP, LUMP)
        sum_send[pl.ds(m * LUMP, LUMP), :] = weighted(m * LUMP, (1 - x_lo) * 512).astype(BF16)
        sum_copy(m).start()
        return carry

    lax.fori_loop(0, LUMPS, partner_half, 0)

    for r in range(8):
        count_src[r : r + 1, :] = to_row(count[pl.ds(r * 128, 128), :])
    count_copy.start()

    def own_half(m, carry):
        own_sum[pl.ds(m * LUMP, LUMP), :] = weighted(m * LUMP, x_lo * 512)
        return carry

    lax.fori_loop(0, LUMPS, own_half, 0)

    def sq_copy(m):
        return remote(sq_src.at[m], sq_dst.at[m], sq_send.at[m], sq_recv.at[m], x_pair)

    def out_copies(m):
        at = pl.ds(m * LUMP, LUMP)
        place = pl.ds(core * 1024 + m * LUMP, LUMP)
        local = pltpu.make_async_copy(
            final.at[at, pl.ds(pl.multiple_of(core * 256, 256), 256)], out_hbm.at[place], out_sem.at[m]
        )
        away = remote(
            final.at[at, pl.ds(pl.multiple_of(other * 256, 256), 256)],
            out_hbm.at[place],
            out_send.at[m],
            out_recv.at[m],
            sibling,
        )
        return local, away

    def finish(m):
        at = pl.ds(m * LUMP, LUMP)
        sum_copy(m).wait_recv()
        total = own_sum[at, :] + sum_recv[at, :].astype(F32)
        own_sum[at, :] = total
        squares = total * total
        lanes = squares[:, :128] + squares[:, 128:256] + squares[:, 256:384] + squares[:, 384:]
        sq_src[m] = jnp.concatenate(
            [to_row(lanes[i * 128 : (i + 1) * 128]) for i in range(LUMP // 128)]
            + [jnp.zeros((8 - LUMP // 128, 128), F32)],
            axis=0,
        )
        sq_copy(m).start()

    def normalize(m):
        sq_copy(m).wait_recv()
        for i in range(LUMP // 128):
            at = pl.ds(m * LUMP + i * 128, 128)
            squares = sq_src[m, i : i + 1, :] + sq_dst[m, i : i + 1, :]
            factor = jnp.broadcast_to(lax.rsqrt(squares + 1e-06), (128, 128)).T
            for tile in range(4):
                lanes = pl.ds(tile * 128, 128)
                final[at, lanes] = (own_sum[at, lanes] * factor).astype(BF16)
        local, away = out_copies(m)
        local.start()
        away.start()

    def last(m, carry):
        pl.when(m < LUMPS)(lambda: finish(m))
        pl.when(m > 0)(lambda: normalize(m - 1))
        return carry

    lax.fori_loop(0, LUMPS + 1, last, 0)

    count_copy.wait_recv()
    mine = pl.ds(pl.multiple_of(core * 8, 8), 8)
    count_all[mine, :] = count_src[...] + count_dst[...]
    all_copy = remote(count_all.at[mine], count_all.at[mine], all_send, all_recv, sibling)
    all_copy.start()

    pre.wait_send()
    wait_bytes(rows.at[pl.ds(0, (SLOTS - 1) * (OWN + EARLY))], row_send)
    wait_bytes(rows.at[pl.ds(0, SLOTS * NODE)], sib_send)
    wait_bytes(rows.at[pl.ds(0, SLOTS * (OWN - EARLY))], late_send)
    wait_bytes(part_dst.at[pl.ds(1, 4 * SLOTS - 1)], part_send)
    wait_bytes(inv.at[pl.ds(1, 2 * SLOTS - 1)], inv_send)
    count_copy.wait_send()
    for m in range(LUMPS):
        sum_copy(m).wait_send()
        sq_copy(m).wait_send()
        local, away = out_copies(m)
        local.wait()
        away.wait()
    all_copy.wait()
    count_out[...] = count_all[...]


def place_results(new_ref, count_ref, log_ref, new_out, count_out, log_out):
    new_out[...] = new_ref[...]
    count_out[...] = count_ref[...]
    log_out[...] = log_ref[:, :OWN]


def on_device(embeddings, centroids):
    dma = pltpu.SemaphoreType.DMA
    any_space = pl.BlockSpec(memory_space=pl.ANY)
    vmem = pl.BlockSpec(memory_space=pltpu.VMEM)
    quarter = pl.BlockSpec((512, 256), lambda i: (i, 0))

    def whole(*shape):
        return pl.BlockSpec(shape, lambda i: (0, 0))

    new_centroids, counts, logs = pl.pallas_call(
        kernel,
        out_shape=(
            jax.ShapeDtypeStruct((2048, 256), BF16),
            jax.ShapeDtypeStruct((16, 128), F32),
            jax.ShapeDtypeStruct((1, 128), F32),
        ),
        in_specs=[any_space, any_space],
        out_specs=(any_space, vmem, vmem),
        scratch_shapes=[
            pltpu.VMEM((ROWS, 1024), BF16),
            pltpu.VMEM((1024, ROWS), BF16),
            pltpu.VMEM((1024, 1024), BF16),
            pltpu.VMEM((OWN, 1024), BF16),
            pltpu.VMEM((1024, 512), F32),
            pltpu.VMEM((1024, 512), BF16),
            pltpu.VMEM((1024, 512), BF16),
            pltpu.VMEM((1024, 512), BF16),
            pltpu.VMEM((2 * SLOTS, 1, PART), F32),
            pltpu.VMEM((4 * SLOTS, 1, PART), F32),
            pltpu.VMEM((2 * SLOTS, 1, PART), F32),
            pltpu.VMEM((1, PART), F32),
            pltpu.VMEM((1, ROWS), F32),
            pltpu.VMEM((1024, 128), F32),
            pltpu.VMEM((8, 128), F32),
            pltpu.VMEM((8, 128), F32),
            pltpu.VMEM((16, 128), F32),
            pltpu.VMEM((LUMPS, 8, 128), F32),
            pltpu.VMEM((LUMPS, 8, 128), F32),
            dma((2,)),
            dma, dma((SLOTS, 2)),
            dma, dma((SLOTS, 2)),
            dma, dma,
            dma, dma((SLOTS,)),
            dma, dma,
            dma, dma,
            dma((LUMPS,)), dma((LUMPS,)),
            dma, dma,
            dma((LUMPS,)), dma((LUMPS,)),
            dma((LUMPS,)), dma((LUMPS,)), dma((LUMPS,)),
            dma, dma,
        ],
        compiler_params=pltpu.CompilerParams(
            collective_id=0, has_side_effects=True, vmem_limit_bytes=60 * 1024 * 1024
        ),
        name="soft_kmeans",
    )(embeddings, centroids)
    new_centroids, counts, logs = pl.pallas_call(
        place_results,
        out_shape=(
            jax.ShapeDtypeStruct((2048, 256), BF16),
            jax.ShapeDtypeStruct((16, 128), F32),
            jax.ShapeDtypeStruct((1, OWN), F32),
        ),
        grid=(4,),
        in_specs=[quarter, whole(16, 128), whole(1, 128)],
        out_specs=(quarter, whole(16, 128), whole(1, OWN)),
        name="place_results",
    )(new_centroids, counts, logs)
    return new_centroids, counts.reshape(2048), logs.reshape(OWN)


def solution(mesh):
    return jax.shard_map(
        on_device,
        mesh=mesh,
        in_specs=(P(("dp", "comp"), None), P("comp", None)),
        out_specs=(P("comp", "dp"), P("comp"), P(("dp", "comp"))),
        check_vma=False,
    )
```

```python
import jax
import jax.numpy as jnp
from jax import lax
from jax.experimental import pallas as pl
from jax.experimental.pallas import tpu as pltpu
from jax.sharding import PartitionSpec as P

MESH = pl.DeviceIdType.MESH
F32 = jnp.float32
BF16 = jnp.bfloat16

ORDER = (
    (0, 0), (1, 0), (0, 1), (3, 0), (0, 3), (2, 0), (0, 2), (1, 1),
    (3, 3), (1, 3), (3, 1), (2, 1), (1, 2), (2, 3), (3, 2), (2, 2),
)
SLOTS = len(ORDER)
SLOT_OF = {place: slot for slot, place in enumerate(ORDER)}
OWN = 96
EARLY = 64
NODE = 2 * OWN
HALVES = ((0, OWN), (OWN, EARLY))
STEP = 2 * NODE
ROWS = SLOTS * STEP
LEAD = 3
PART = 256
LUMP = 256
LUMPS = 1024 // LUMP


def children(slot, half):
    place = ORDER[slot]
    first, second = place if half == 0 else place[::-1]
    found = []
    if second == 0:
        if first == 0:
            found += [((1, 0), 0, 1), ((3, 0), 0, -1)]
        if first == 1:
            found += [((2, 0), 0, 1)]
        found += [((first, 1), 1, 1), ((first, 3), 1, -1)]
    elif second == 1 and first in (0, 1):
        found += [((first, 2), 1, 1)]
    elif second == 3 and first in (2, 3):
        found += [((first, 2), 1, -1)]
    if half == 0:
        return [(SLOT_OF[p], axis, way) for p, axis, way in found]
    return [(SLOT_OF[p[::-1]], 1 - axis, way) for p, axis, way in found]


def choose(index, low, high, work):
    if high - low == 1:
        work(low)
        return
    middle = (low + high) // 2
    pl.when(index < middle)(lambda: choose(index, low, middle, work))
    pl.when(index >= middle)(lambda: choose(index, middle, high, work))


def kernel(
    emb_hbm, cent_hbm, out_hbm, count_out, log_out,
    rows, probs, cent, emb, own_sum, sum_send, sum_recv, final,
    part_src, part_dst, inv, inv_src, inv_row, count, count_src, count_dst, count_all, sq_src, sq_dst,
    load_sem, row_send, row_recv, sib_send, sib_recv, pre_send, pre_recv, late_send, late_recv,
    part_send, part_recv, inv_send, inv_recv,
    sum_ssem, sum_rsem, cnt_send, cnt_recv, sq_send, sq_recv, out_sem, out_send, out_recv, all_send, all_recv,
):
    dp = lax.axis_index("dp")
    comp = lax.axis_index("comp")
    core = lax.rem(dp, 2)
    other = 1 - core
    x_lo = dp // 2
    y = lax.rem(comp, 4)
    x = lax.rem(comp // 4, 2) * 2 + x_lo
    z = comp // 8
    sign = 1 - 2 * core

    at_y = [lax.rem(y + sign * d + 4, 4) for d in range(4)]
    at_z = [lax.rem(z + sign * d + 4, 4) * 8 for d in range(4)]
    at_first = [y_id * other + z_id * core for y_id, z_id in zip(at_y, at_z)]
    at_second = [y_id * core + z_id * other for y_id, z_id in zip(at_y, at_z)]
    at_x = [lax.rem(x + d, 4) for d in range(4)]
    at_x_comp = [(place // 2) * 4 for place in at_x]
    at_x_dp = [lax.rem(place, 2) * 2 for place in at_x]
    cores = (core, other)

    def device(dx, first, second, dcore):
        comp_id = at_first[first % 4] + at_x_comp[dx % 4] + at_second[second % 4]
        return {"dp": at_x_dp[dx % 4] + cores[dcore], "comp": comp_id}

    def remote(src, dst, ssem, rsem, target):
        return pltpu.make_async_remote_copy(
            src_ref=src, dst_ref=dst, send_sem=ssem, recv_sem=rsem, device_id=target, device_id_type=MESH
        )

    def wait_bytes(ref, sem):
        pltpu.make_async_copy(ref, ref, sem).wait()

    sibling = device(0, 0, 0, 1)
    x_far = device(2, 0, 0, 0)
    x_pair = {"dp": (1 - x_lo) * 2 + core, "comp": comp}

    emb_copy = pltpu.make_async_copy(emb_hbm, emb, load_sem.at[0])
    emb_copy.start()
    cent_copy = pltpu.make_async_copy(cent_hbm.at[pl.ds(core * 1024, 1024)], cent, load_sem.at[1])
    cent_copy.start()

    barrier = pltpu.get_barrier_semaphore()
    greeted = 0
    for place in ORDER:
        for dcore in (0, 1):
            if (*place, dcore) != (0, 0, 0):
                pl.semaphore_signal(barrier, inc=1, device_id=device(0, *place, dcore), device_id_type=MESH)
                greeted += 1
            pl.semaphore_signal(barrier, inc=1, device_id=device(2, *place, dcore), device_id_type=MESH)
            greeted += 1
    for dx in (1, 3):
        pl.semaphore_signal(barrier, inc=1, device_id=device(dx, 0, 0, 0), device_id_type=MESH)
        greeted += 1

    def unit(values):
        floats = values.astype(F32)
        return (floats * lax.rsqrt(jnp.sum(floats * floats, axis=1, keepdims=True) + 1e-06)).astype(BF16)

    emb_copy.wait()
    rows[pl.ds(0, OWN), :] = unit(emb[...])
    pl.semaphore_wait(barrier, greeted)

    pre = remote(rows.at[pl.ds(0, EARLY)], rows.at[pl.ds(OWN, EARLY)], pre_send, pre_recv, x_far)
    pre.start()

    def row_copy(slot, half, child, axis, way):
        first, second = (way, 0) if axis == 0 else (0, way)
        start, size = HALVES[half]
        return remote(
            rows.at[pl.ds(slot * STEP + start, size)],
            rows.at[pl.ds(child * STEP + start, size)],
            row_send,
            row_recv.at[child, half],
            device(0, first, second, 0),
        )

    def hand_on(slot, half):
        for child, axis, way in children(slot, half):
            row_copy(slot, half, child, axis, way).start()

    def late_copy(slot):
        at = slot * STEP
        return remote(
            rows.at[pl.ds(at + EARLY, OWN - EARLY)],
            rows.at[pl.ds(at + OWN + EARLY, OWN - EARLY)],
            late_send,
            late_recv.at[slot],
            x_far,
        )

    def to_sibling(slot, late):
        first, size = (OWN + EARLY, OWN - EARLY) if late else (0, OWN + EARLY)
        at = slot * STEP + first
        return remote(
            rows.at[pl.ds(at, size)], rows.at[pl.ds(at + NODE, size)], sib_send, sib_recv.at[slot, late], sibling
        )

    def arrive(slot):
        row_copy(slot, 0, slot, 0, 1).wait_recv()
        hand_on(slot, 0)
        late_copy(slot).start()
        row_copy(slot, 1, slot, 0, 1).wait_recv()
        hand_on(slot, 1)
        to_sibling(slot, 0).start()

    def arrive_late(slot):
        late_copy(slot).wait_recv()
        to_sibling(slot, 1).start()

    hand_on(0, 0)
    pre.wait_recv()
    hand_on(0, 1)
    late_copy(0).start()
    to_sibling(0, 0).start()

    cent_copy.wait()

    def unit_block(i, carry):
        block = pl.ds(i * 128, 128)
        cent[block, :] = unit(cent[block, :])
        return carry

    lax.fori_loop(0, 8, unit_block, 0)
    def score(slot):
        at = pl.ds((slot - 1) * STEP, 2 * STEP)
        scores = lax.dot_general(cent[...], rows[at, :], (((1,), (1,)), ((), ())), preferred_element_type=F32)
        p = jnp.exp(scores * 10.0 - 10.0)
        probs[:, at] = p.astype(BF16)
        part = jnp.sum(p, axis=0, keepdims=True)
        for i in (0, 1):
            node = part[:, i * STEP : (i + 1) * STEP]
            part_src[2 * (slot - 1 + i)] = node[:, :PART]
            part_src[2 * (slot - 1 + i) + 1] = pltpu.roll(node, STEP - NODE, 1)[:, :PART]

    def send_part(slot):
        first, second = ORDER[slot]
        for dcore, place in ((0, (-first, -second)), (1, (second, first))):
            tile = 2 * slot + dcore
            for dx, base in ((0, 0), (2, 2 * SLOTS)):
                if dx + tile == 0:
                    part_dst[0] = part_src[0]
                else:
                    remote(
                        part_src.at[tile], part_dst.at[base + tile], part_send, part_recv, device(dx, *place, dcore)
                    ).start()

    def totals_first():
        wait_bytes(part_dst.at[pl.ds(1, 4 * SLOTS - 1)], part_recv)
        near = jnp.sum(part_dst[pl.ds(0, 2 * SLOTS)], axis=0)
        far = jnp.sum(part_dst[pl.ds(2 * SLOTS, 2 * SLOTS)], axis=0)
        lane = lax.broadcasted_iota(jnp.int32, (1, PART), 1)
        total = near + jnp.where(lane < OWN, pltpu.roll(far, PART - OWN, 1), pltpu.roll(far, OWN, 1))
        total = jnp.where(lane < NODE, total, 1.0)
        inv_src[...] = 1.0 / total
        inv[0] = 1.0 / total
        for slot in reversed(range(SLOTS)):
            place = ORDER[slot]
            for dcore in (0, 1):
                if slot + dcore > 0:
                    remote(
                        inv_src, inv.at[2 * slot + dcore], inv_send, inv_recv, device(0, *place, dcore)
                    ).start()
        log_out[...] = jnp.log(total[:, :128]) + 10.0

    def totals_second():
        wait_bytes(inv.at[pl.ds(1, 2 * SLOTS - 1)], inv_recv)
        lane = lax.broadcasted_iota(jnp.int32, (1, STEP), 1)
        rest = jnp.zeros((1, STEP - PART), F32)
        for slot in range(SLOTS):
            mine = jnp.concatenate([inv[2 * slot], rest], axis=1)
            theirs = pltpu.roll(jnp.concatenate([inv[2 * slot + 1], rest], axis=1), NODE, 1)
            inv_row[:, pl.ds(slot * STEP, STEP)] = jnp.where(lane < NODE, mine, theirs)

    def scale(start, size):
        def block(i, carry):
            at = pl.ds(start + i * 64, 64)
            total = jnp.zeros((64, 128), F32)
            for tile in range(ROWS // 128):
                lanes = pl.ds(tile * 128, 128)
                weights = (probs[at, lanes].astype(F32) * inv_row[:, lanes]).astype(BF16)
                probs[at, lanes] = weights
                total = total + weights.astype(F32)
            count[at, :] = total
            return carry

        lax.fori_loop(0, size // 64, block, 0)

    def to_row(block):
        return jnp.sum(block.T, axis=0, keepdims=True)

    def weighted(start, column, size=LUMP):
        return lax.dot_general(
            probs[pl.ds(start, size), :],
            rows[:, pl.ds(column, 512)],
            (((1,), (0,)), ((), ())),
            preferred_element_type=F32,
        )

    def sum_copy(m):
        at = pl.ds(m * LUMP, LUMP)
        return remote(sum_send.at[at], sum_recv.at[at], sum_ssem.at[m], sum_rsem.at[m], x_pair)

    count_copy = remote(count_src, count_dst, cnt_send, cnt_recv, x_pair)

    def step(t, carry):
        @pl.when(t < SLOTS - LEAD)
        def _():
            choose(t + LEAD, LEAD, SLOTS, arrive)

        @pl.when(t < SLOTS - 1)
        def _():
            arrive_late(t + 1)

        @pl.when(lax.rem(t, 2) == 1)
        def _():
            for slot in (t - 1, t):
                for late in (0, 1):
                    to_sibling(slot, late).wait_recv()
            score(t)
            choose(t // 2, 0, SLOTS // 2, lambda k: (send_part(2 * k), send_part(2 * k + 1)))

        return carry

    for slot in range(1, LEAD):
        arrive(slot)
    arrive_late(0)
    lax.fori_loop(0, SLOTS, step, 0)
    totals_first()
    totals_second()

    def partner_sums(start, size, m):
        at = pl.ds(start, size)
        scale(start, size)
        sum_send[at, :] = weighted(start, (1 - x_lo) * 512, size).astype(BF16)
        remote(sum_send.at[at], sum_recv.at[at], sum_ssem.at[m], sum_rsem.at[m], x_pair).start()

    def first_lump(i, carry):
        partner_sums(i * (LUMP // 2), LUMP // 2, 0)
        return carry

    def partner_half(m, carry):
        partner_sums(m * LUMP, LUMP, m)
        return carry

    lax.fori_loop(0, 2, first_lump, 0)
    lax.fori_loop(1, LUMPS, partner_half, 0)

    for r in range(8):
        count_src[r : r + 1, :] = to_row(count[pl.ds(r * 128, 128), :])
    count_copy.start()

    def own_half(m, carry):
        own_sum[pl.ds(m * LUMP, LUMP), :] = weighted(m * LUMP, x_lo * 512)
        return carry

    lax.fori_loop(0, LUMPS, own_half, 0)

    def sq_copy(m):
        return remote(sq_src.at[m], sq_dst.at[m], sq_send.at[m], sq_recv.at[m], x_pair)

    def out_copies(m):
        at = pl.ds(m * LUMP, LUMP)
        place = pl.ds(core * 1024 + m * LUMP, LUMP)
        local = pltpu.make_async_copy(
            final.at[at, pl.ds(pl.multiple_of(core * 256, 256), 256)], out_hbm.at[place], out_sem.at[m]
        )
        away = remote(
            final.at[at, pl.ds(pl.multiple_of(other * 256, 256), 256)],
            out_hbm.at[place],
            out_send.at[m],
            out_recv.at[m],
            sibling,
        )
        return local, away

    def finish(m):
        at = pl.ds(m * LUMP, LUMP)
        sum_copy(m).wait_recv()
        total = own_sum[at, :] + sum_recv[at, :].astype(F32)
        own_sum[at, :] = total
        squares = total * total
        lanes = squares[:, :128] + squares[:, 128:256] + squares[:, 256:384] + squares[:, 384:]
        sq_src[m] = jnp.concatenate(
            [to_row(lanes[i * 128 : (i + 1) * 128]) for i in range(LUMP // 128)]
            + [jnp.zeros((8 - LUMP // 128, 128), F32)],
            axis=0,
        )
        sq_copy(m).start()

    def normalize(m):
        sq_copy(m).wait_recv()
        for i in range(LUMP // 128):
            at = pl.ds(m * LUMP + i * 128, 128)
            squares = sq_src[m, i : i + 1, :] + sq_dst[m, i : i + 1, :]
            factor = jnp.broadcast_to(lax.rsqrt(squares + 1e-06), (128, 128)).T
            for tile in range(4):
                lanes = pl.ds(tile * 128, 128)
                final[at, lanes] = (own_sum[at, lanes] * factor).astype(BF16)
        local, away = out_copies(m)
        local.start()
        away.start()

    def last(m, carry):
        pl.when(m < LUMPS)(lambda: finish(m))
        pl.when(m > 0)(lambda: normalize(m - 1))
        return carry

    lax.fori_loop(0, LUMPS + 1, last, 0)

    count_copy.wait_recv()
    mine = pl.ds(pl.multiple_of(core * 8, 8), 8)
    count_all[mine, :] = count_src[...] + count_dst[...]
    all_copy = remote(count_all.at[mine], count_all.at[mine], all_send, all_recv, sibling)
    all_copy.start()

    pre.wait_send()
    wait_bytes(rows.at[pl.ds(0, (SLOTS - 1) * (OWN + EARLY))], row_send)
    wait_bytes(rows.at[pl.ds(0, SLOTS * NODE)], sib_send)
    wait_bytes(rows.at[pl.ds(0, SLOTS * (OWN - EARLY))], late_send)
    wait_bytes(part_dst.at[pl.ds(1, 4 * SLOTS - 1)], part_send)
    wait_bytes(inv.at[pl.ds(1, 2 * SLOTS - 1)], inv_send)
    count_copy.wait_send()
    for m in range(LUMPS):
        sum_copy(m).wait_send()
        sq_copy(m).wait_send()
        local, away = out_copies(m)
        local.wait()
        away.wait()
    all_copy.wait()
    count_out[...] = count_all[...]


def place_results(new_ref, count_ref, log_ref, new_out, count_out, log_out):
    new_out[...] = new_ref[...]
    count_out[...] = count_ref[...]
    log_out[...] = log_ref[:, :OWN]


def on_device(embeddings, centroids):
    dma = pltpu.SemaphoreType.DMA
    any_space = pl.BlockSpec(memory_space=pl.ANY)
    vmem = pl.BlockSpec(memory_space=pltpu.VMEM)
    quarter = pl.BlockSpec((512, 256), lambda i: (i, 0))

    def whole(*shape):
        return pl.BlockSpec(shape, lambda i: (0, 0))

    new_centroids, counts, logs = pl.pallas_call(
        kernel,
        out_shape=(
            jax.ShapeDtypeStruct((2048, 256), BF16),
            jax.ShapeDtypeStruct((16, 128), F32),
            jax.ShapeDtypeStruct((1, 128), F32),
        ),
        in_specs=[any_space, any_space],
        out_specs=(any_space, vmem, vmem),
        scratch_shapes=[
            pltpu.VMEM((ROWS, 1024), BF16),
            pltpu.VMEM((1024, ROWS), BF16),
            pltpu.VMEM((1024, 1024), BF16),
            pltpu.VMEM((OWN, 1024), BF16),
            pltpu.VMEM((1024, 512), F32),
            pltpu.VMEM((1024, 512), BF16),
            pltpu.VMEM((1024, 512), BF16),
            pltpu.VMEM((1024, 512), BF16),
            pltpu.VMEM((2 * SLOTS, 1, PART), F32),
            pltpu.VMEM((4 * SLOTS, 1, PART), F32),
            pltpu.VMEM((2 * SLOTS, 1, PART), F32),
            pltpu.VMEM((1, PART), F32),
            pltpu.VMEM((1, ROWS), F32),
            pltpu.VMEM((1024, 128), F32),
            pltpu.VMEM((8, 128), F32),
            pltpu.VMEM((8, 128), F32),
            pltpu.VMEM((16, 128), F32),
            pltpu.VMEM((LUMPS, 8, 128), F32),
            pltpu.VMEM((LUMPS, 8, 128), F32),
            dma((2,)),
            dma, dma((SLOTS, 2)),
            dma, dma((SLOTS, 2)),
            dma, dma,
            dma, dma((SLOTS,)),
            dma, dma,
            dma, dma,
            dma((LUMPS,)), dma((LUMPS,)),
            dma, dma,
            dma((LUMPS,)), dma((LUMPS,)),
            dma((LUMPS,)), dma((LUMPS,)), dma((LUMPS,)),
            dma, dma,
        ],
        compiler_params=pltpu.CompilerParams(
            collective_id=0, has_side_effects=True, vmem_limit_bytes=60 * 1024 * 1024
        ),
        name="soft_kmeans",
    )(embeddings, centroids)
    new_centroids, counts, logs = pl.pallas_call(
        place_results,
        out_shape=(
            jax.ShapeDtypeStruct((2048, 256), BF16),
            jax.ShapeDtypeStruct((16, 128), F32),
            jax.ShapeDtypeStruct((1, OWN), F32),
        ),
        grid=(4,),
        in_specs=[quarter, whole(16, 128), whole(1, 128)],
        out_specs=(quarter, whole(16, 128), whole(1, OWN)),
        name="place_results",
    )(new_centroids, counts, logs)
    return new_centroids, counts.reshape(2048), logs.reshape(OWN)


def solution(mesh):
    return jax.shard_map(
        on_device,
        mesh=mesh,
        in_specs=(P(("dp", "comp"), None), P("comp", None)),
        out_specs=(P("comp", "dp"), P("comp"), P(("dp", "comp"))),
        check_vma=False,
    )
```
